32 devices in a mesh: dev: 32 (over z, y, x, core).
Axes of the slice: x: 2, y: 2, z: 4, core: 2. Of those that a mesh axis runs over, the one named last changes fastest.
Arguments:
- velocity: float32 [256, 64, 256], P('dev'), may hold values from 1.5 to 4.5
- wave_prev: float32 [1024, 32, 128], P('dev')
- wave_now: float32 [1024, 32, 128], P('dev')
- adjoint_next: float32 [1024, 32, 128], P('dev'), may hold values from -6 to 6
- adjoint_now: float32 [1024, 32, 128], P('dev'), may hold values from -6 to 6
- wavelet: float32 [32, 2], P('dev'), may hold values from -12 to 12
- source_pos: int32 [32, 3], P('dev'), may hold values from 0 to 31, as said below
- cover_start: int32 [32], replicated, may hold values from 0 to 28, as said below
- lateral_anchor: int32 [32, 2], replicated, may hold values from 0 to 128, as said below
Outputs:
- wave_last: float32 [1024, 32, 128], P('dev')
- adjoint_last: float32 [1024, 32, 128], P('dev')
- gradient: float32 [256, 64, 256], P('dev')
The draws below stay inside these ranges and needn't reach their ends.
Inputs may be any that keep to these rules, and one draw needn't show every extreme that they name: Aperture a covers the 4 slabs from cover_start[a] on, and its own slab a is among them. `lateral_anchor`: first entry at most 32, second at most 128. `source_pos`: every coordinate is below the smallest of 32, 32 and 128.
All inputs are finite; a program needn't handle non-finite values. Where the reference program divides by a largest or mean magnitude, that divisor is 1e-20 or more.
Results may differ from the reference program's by a relative error of at most 0.00002.
Values sent between devices are 32-bit elements; how exact they have to be, the bound alone decides.
A program may use at most 64 MiB of HBM per device.

```python
import jax
import jax.numpy as jnp
from jax import lax

SLAB = 8
K = 4
AX = 32
AY = 128
AZ = 32
MX = 64
MY = 256
OWNERS = 32
DEPTH = 256
ROWS = 1024
N_DEV = 32


def wave_field(key):
    shape_full = (N_DEV, AZ, AX, AY)
    rising = jnp.power(jnp.float32(3.0), jnp.arange(N_DEV, dtype=jnp.float32) / (N_DEV - 1))
    base = jax.random.normal(jax.random.fold_in(key, 3), shape_full, jnp.float32)
    scales = rising
    return (base * scales[:, None, None, None]).reshape(N_DEV * AZ, AX, AY).astype(jnp.float32)


def draw_wave_prev(key, part):
    return wave_field(jax.random.fold_in(key, 11))


def draw_wave_now(key, part):
    return wave_field(jax.random.fold_in(key, 12))


def draw_cover_start(key, part):
    lagging = jax.random.randint(jax.random.fold_in(key, 21), (N_DEV,), 0, K)
    starting = jnp.arange(N_DEV, dtype=jnp.int32) - lagging
    return jnp.clip(starting, 0, N_DEV - K).astype(jnp.int32)


def draw_lateral_anchor(key, part):
    crossing = jax.random.randint(jax.random.fold_in(key, 31), (N_DEV,), 0, AX + 1)
    alongside = jax.random.randint(jax.random.fold_in(key, 32), (N_DEV,), 0, AY + 1)
    anchors = jnp.stack([crossing, alongside], 1).astype(jnp.int32)
    anchors = anchors.at[0].set(jnp.array([0, 0], jnp.int32))
    anchors = anchors.at[N_DEV - 1].set(jnp.array([AX, AY], jnp.int32))
    return anchors


def draw_source_pos(key, part):
    bounded = min(AZ, min(AX, AY))
    positions = jax.random.randint(jax.random.fold_in(key, 41), (N_DEV, 3), 0, bounded).astype(jnp.int32)
    positions = positions.at[0].set(jnp.array([0, 0, bounded - 1], jnp.int32))
    return positions


def block_levels(own_key, shape, split, smallest, top_value):
    def one(axis_at, blocks):
        steps = jax.random.uniform(jax.random.fold_in(jax.random.fold_in(own_key, 6), axis_at), (blocks,), jnp.float32, smallest / len(split), top_value / len(split))
        return jnp.repeat(jnp.exp(steps), shape[axis_at] // blocks).reshape((-1,) + (1,) * (len(shape) - axis_at - 1))

    gain = one(*split[0])
    for cut in split[1:]:
        gain = gain * one(*cut)
    return gain


def bell_draw(key, extent, width, limit, shards=(), kind=jnp.bfloat16):
    level = block_levels(key, extent, shards, -0.22, 0.18) if shards else 1.0
    entries = jax.random.normal(key, extent, jnp.float32) * width * level
    return jnp.minimum(jnp.maximum(entries, -limit), limit).astype(kind)


def setup_inputs(seed: int = 0) -> dict:
    streams_of = jax.random.split(jax.random.key(seed), 10)
    velocity = jnp.clip(1.5 + 3.0 * jax.random.uniform(streams_of[0], (DEPTH, MX, MY), jnp.float32) ** block_levels(streams_of[0], (DEPTH, MX, MY), ((0, 32),), -0.2, 0.2), 1.5, 4.5)
    wave_prev = draw_wave_prev(jax.random.fold_in(streams_of[9], 71), 0)
    wave_now = draw_wave_now(jax.random.fold_in(streams_of[9], 71), 0)
    adjoint_next = bell_draw(streams_of[3], (ROWS, AX, AY), 1.0, 6.0, ((0, 32),), jnp.float32)
    adjoint_now = bell_draw(streams_of[4], (ROWS, AX, AY), 1.0, 6.0, ((0, 32),), jnp.float32)
    wavelet = bell_draw(streams_of[5], (OWNERS, 2), 3.0, 12.0, ((0, 32),), jnp.float32)
    source_pos = draw_source_pos(jax.random.fold_in(streams_of[9], 71), 0)
    cover_start = draw_cover_start(jax.random.fold_in(streams_of[9], 71), 0)
    lateral_anchor = draw_lateral_anchor(jax.random.fold_in(streams_of[9], 71), 0)
    return {"velocity": velocity, "wave_prev": wave_prev, "wave_now": wave_now, "adjoint_next": adjoint_next, "adjoint_now": adjoint_now, "wavelet": wavelet, "source_pos": source_pos, "cover_start": cover_start, "lateral_anchor": lateral_anchor}


STENCIL_WEIGHTS = (-205.0 / 72.0, 8.0 / 5.0, -1.0 / 5.0, 8.0 / 315.0, -1.0 / 560.0)
STEP_RATIO = 0.088
EPSILON = 1e-6


def laplace(wavefield):
    depth_cells, cross_cells, along_cells = wavefield.shape
    padded = jnp.pad(wavefield, 4)
    summed = (3.0 * STENCIL_WEIGHTS[0]) * wavefield
    for distance in range(1, 5):
        weight = STENCIL_WEIGHTS[distance]
        summed = summed + weight * (padded[4 + distance:4 + distance + depth_cells, 4:4 + cross_cells, 4:4 + along_cells] + padded[4 - distance:4 - distance + depth_cells, 4:4 + cross_cells, 4:4 + along_cells])
        summed = summed + weight * (padded[4:4 + depth_cells, 4 + distance:4 + distance + cross_cells, 4:4 + along_cells] + padded[4:4 + depth_cells, 4 - distance:4 - distance + cross_cells, 4:4 + along_cells])
        summed = summed + weight * (padded[4:4 + depth_cells, 4:4 + cross_cells, 4 + distance:4 + distance + along_cells] + padded[4:4 + depth_cells, 4:4 + cross_cells, 4 - distance:4 - distance + along_cells])
    return summed


def aperture_step(aperture_speed, wave_zero, wave_one, adjoint_four, adjoint_three, wavelet_pair, position):
    courant = jnp.square(aperture_speed * STEP_RATIO)
    shape_full = wave_zero.shape
    depth_hit = lax.broadcasted_iota(jnp.int32, shape_full, 0) == position[0].astype(jnp.int32)
    cross_hit = lax.broadcasted_iota(jnp.int32, shape_full, 1) == position[1].astype(jnp.int32)
    along_hit = lax.broadcasted_iota(jnp.int32, shape_full, 2) == position[2].astype(jnp.int32)
    source_mask = jnp.where(depth_hit & cross_hit & along_hit, jnp.float32(1.0), jnp.float32(0.0))
    laplace_zero = laplace(wave_zero)
    laplace_one = laplace(wave_one)
    wave_two = 2.0 * wave_one - wave_zero + courant * laplace_one + wavelet_pair[0] * source_mask
    laplace_two = laplace(wave_two)
    wave_three = 2.0 * wave_two - wave_one + courant * laplace_two + wavelet_pair[1] * source_mask
    laplace_three = laplace(wave_three)
    adjoint_two = 2.0 * adjoint_three - adjoint_four + laplace(courant * adjoint_three)
    adjoint_one = 2.0 * adjoint_two - adjoint_three + laplace(courant * adjoint_two)
    grad_courant = adjoint_one * laplace_zero + adjoint_two * laplace_one + adjoint_three * laplace_two + adjoint_four * laplace_three
    return wave_three, adjoint_one, grad_courant


def reference(velocity, wave_prev, wave_now, adjoint_next, adjoint_now, wavelet, source_pos, cover_start, lateral_anchor):
    def accumulate(aperture, carried):
        grad_sum, wave_out, adjoint_out = carried
        aperture = jnp.asarray(aperture).astype(jnp.int32)
        depth_start = (cover_start[aperture] * SLAB).astype(jnp.int32)
        anchor_cross = lateral_anchor[aperture, 0].astype(jnp.int32)
        anchor_along = lateral_anchor[aperture, 1].astype(jnp.int32)
        row_start = (aperture * AZ).astype(jnp.int32)

        def cut_rows(array):
            return lax.dynamic_slice_in_dim(array, row_start, AZ, 0)

        aperture_speed = lax.dynamic_slice(velocity, (depth_start, anchor_cross, anchor_along), (AZ, AX, AY))
        wave_three, adjoint_one, grad_courant = aperture_step(aperture_speed, cut_rows(wave_prev), cut_rows(wave_now), cut_rows(adjoint_next), cut_rows(adjoint_now), wavelet[aperture], source_pos[aperture])
        region = lax.dynamic_slice(grad_sum, (depth_start, anchor_cross, anchor_along), (AZ, AX, AY))
        grad_sum = lax.dynamic_update_slice(grad_sum, region + grad_courant, (depth_start, anchor_cross, anchor_along))
        wave_out = lax.dynamic_update_slice_in_dim(wave_out, wave_three, row_start, 0)
        adjoint_out = lax.dynamic_update_slice_in_dim(adjoint_out, adjoint_one, row_start, 0)
        return grad_sum, wave_out, adjoint_out

    initial = (jnp.zeros(velocity.shape, jnp.float32), jnp.zeros(wave_prev.shape, jnp.float32), jnp.zeros(wave_prev.shape, jnp.float32))
    grad_sum, wave_out, adjoint_out = lax.fori_loop(0, N_DEV, accumulate, initial)
    speed_grad = (2.0 * STEP_RATIO * STEP_RATIO) * velocity * grad_sum
    peak_value = jnp.max(jnp.abs(speed_grad))
    gradient = speed_grad / (peak_value + EPSILON)
    return wave_out, adjoint_out, gradient
```

```python
import functools

import jax
import jax.numpy as jnp
from jax import lax
from jax.experimental import pallas as pl
from jax.experimental.pallas import tpu as pltpu
from jax.sharding import PartitionSpec as P

SLAB = 8
K = 4
AX = 32
AY = 128
AZ = 32

WEIGHTS = (-205.0 / 72.0, 8.0 / 5.0, -1.0 / 5.0, 8.0 / 315.0, -1.0 / 560.0)
STEP_RATIO = 0.088
EPSILON = 1e-06
REACH = K - 1
SLOTS = 2 * REACH + 1
OFFSETS = (3, -3, 2, -2, 1, -1)
MESH = pl.DeviceIdType.MESH


def stages_of(count):
    stages, stride = [], 1
    while stride < count:
        left = count // stride
        radix = max(r for r in range(2, max(9, left + 1)) if left % r == 0 and (r <= 8 or r == left))
        if radix > 8:
            radix = next((r for r in range(8, 1, -1) if left % r == 0), left)
        stages.append((stride, radix))
        stride *= radix
    return stages


def kernel(
    n,
    stages,
    vel,
    prev_in,
    now_in,
    adj4_in,
    adj3_in,
    wavelet,
    spos,
    cover,
    anchor,
    wave_out,
    adj_out,
    grad_out,
    pad0,
    pad1,
    pad2,
    pad3,
    padc3,
    padc2,
    q4,
    q3,
    q2,
    lap0,
    lap1,
    lap2,
    cour,
    doubled,
    vsend,
    vrecv,
    gsend,
    grecv,
    total,
    mxsend,
    mxrecv,
    in_sem,
    vs_sem,
    vr_sem,
    gs_sem,
    gr_sem,
    ms_sem,
    mr_sem,
):
    me = lax.axis_index("dev")
    barrier = pltpu.get_barrier_semaphore()
    group = stages[0][1]

    def there(d):
        return (me + d >= 0) & (me + d < n)

    def partner(stride, radix, j):
        digit = (me // stride) % radix
        return me + ((digit + j) % radix - digit) * stride

    expected = 0
    for stride, radix in stages:
        for j in range(1, radix):
            pl.semaphore_signal(
                barrier, inc=1, device_id=(partner(stride, radix, j),), device_id_type=MESH
            )
            expected += 1
    for d in OFFSETS:
        outside = there(d) & ((me + d + group) // group != (me + group) // group)

        @pl.when(outside)
        def _(d=d):
            pl.semaphore_signal(barrier, inc=1, device_id=(me + d,), device_id_type=MESH)

        expected = expected + jnp.where(outside, 1, 0)

    loads = [
        pltpu.make_async_copy(prev_in, pad0.at[4:36, 8:40], in_sem.at[0]),
        pltpu.make_async_copy(now_in, pad1.at[4:36, 8:40], in_sem.at[1]),
        pltpu.make_async_copy(adj4_in, q4, in_sem.at[2]),
        pltpu.make_async_copy(adj3_in, q3, in_sem.at[3]),
    ]
    for load in loads:
        load.start()

    rows = lax.broadcasted_iota(jnp.int32, (AX, AY), 0)
    lanes = lax.broadcasted_iota(jnp.int32, (AX, AY), 1)

    def fold(target):
        cross, along = anchor[target, 0], anchor[target, 1]
        low_lane = lanes >= along
        low_row = rows >= cross
        top = jnp.where(low_lane, vel[:, 0:AX, 0:AY], vel[:, 0:AX, AY : 2 * AY])
        bottom = jnp.where(low_lane, vel[:, AX : 2 * AX, 0:AY], vel[:, AX : 2 * AX, AY : 2 * AY])
        return jnp.where(low_row, top, bottom)

    for d in OFFSETS:
        vsend[d + REACH] = fold(jnp.clip(me + d, 0, n - 1))
    vrecv[REACH] = fold(me)

    pl.semaphore_wait(barrier, expected)

    def v_copy(d):
        return pltpu.make_async_remote_copy(
            src_ref=vsend.at[d + REACH],
            dst_ref=vrecv.at[REACH - d],
            send_sem=vs_sem.at[d + REACH],
            recv_sem=vr_sem.at[REACH - d],
            device_id=(me + d,),
            device_id_type=MESH,
        )

    def g_copy(d):
        return pltpu.make_async_remote_copy(
            src_ref=gsend.at[d + REACH],
            dst_ref=grecv.at[REACH - d],
            send_sem=gs_sem.at[d + REACH],
            recv_sem=gr_sem.at[REACH - d],
            device_id=(me + d,),
            device_id_type=MESH,
        )

    for d in OFFSETS:

        @pl.when(there(d))
        def _(d=d):
            v_copy(d).start()

    for ref in (pad0, pad1, pad2, pad3, padc3, padc2):
        side = jnp.zeros((4, 48, AY), jnp.float32)
        ref[0:4] = side
        ref[36:40] = side

    def clear(z, _):
        edge = jnp.zeros((8, AY), jnp.float32)
        for ref in (pad0, pad1, pad2, pad3, padc3, padc2):
            ref[z + 4, 0:8, :] = edge
            ref[z + 4, 40:48, :] = edge
        return 0

    lax.fori_loop(0, AZ, clear, 0)

    lane_row = lax.broadcasted_iota(jnp.int32, (8, AY), 1)
    ups = [jnp.where(lane_row >= k, jnp.float32(WEIGHTS[k]), 0.0) for k in range(1, 5)]
    downs = [jnp.where(lane_row < AY - k, jnp.float32(WEIGHTS[k]), 0.0) for k in range(1, 5)]

    def lap(ref, z):
        parts = []
        for r in range(8, 40, 8):
            centre = ref[z + 4, r : r + 8, :]
            summed = jnp.float32(3.0 * WEIGHTS[0]) * centre
            for k in range(1, 5):
                summed = summed + jnp.float32(WEIGHTS[k]) * (
                    (ref[z + 4 + k, r : r + 8, :] + ref[z + 4 - k, r : r + 8, :])
                    + (ref[z + 4, r + k : r + k + 8, :] + ref[z + 4, r - k : r - k + 8, :])
                )
                summed = summed + (
                    pltpu.roll(centre, k, 1) * ups[k - 1]
                    + pltpu.roll(centre, AY - k, 1) * downs[k - 1]
                )
            parts.append(summed)
        return jnp.concatenate(parts, 0)

    for load in loads:
        load.wait()

    def first(z, _):
        lap0[z] = lap(pad0, z)
        lap1[z] = lap(pad1, z)
        return 0

    lax.fori_loop(0, AZ, first, 0)

    my_cross, my_along = anchor[me, 0], anchor[me, 1]
    lag = jnp.clip(me - cover[me], 0, K - 1)
    back = lax.rem(AY - my_along, AY)
    ahead = lax.rem(my_along, AY)

    for d in OFFSETS:

        @pl.when(there(d))
        def _(d=d):
            v_copy(-d).wait_recv()

    for k in range(K):
        piece = vrecv[REACH - lag + k]
        speed = pltpu.roll(piece.reshape(SLAB * AX, AY), back, 1) * jnp.float32(STEP_RATIO)
        speed = (speed * speed).reshape(SLAB, AX, AY)
        doubled[SLAB * k : SLAB * (k + 1), 0:AX, :] = speed
        doubled[SLAB * k : SLAB * (k + 1), AX : 2 * AX, :] = speed

    plane_hit = (rows == spos[0, 1]) & (lanes == spos[0, 2])
    plane_one = jnp.where(plane_hit, wavelet[0, 0], 0.0)
    plane_two = jnp.where(plane_hit, wavelet[0, 1], 0.0)
    source_depth = spos[0, 0]

    def second(z, _):
        c = doubled[z, pl.ds(my_cross, AX), :]
        cour[z] = c
        hit = jnp.where(source_depth == z, jnp.float32(1.0), jnp.float32(0.0))
        pad2[z + 4, 8:40, :] = (
            2.0 * pad1[z + 4, 8:40, :] - pad0[z + 4, 8:40, :] + c * lap1[z] + hit * plane_one
        )
        padc3[z + 4, 8:40, :] = c * q3[z]
        return 0

    lax.fori_loop(0, AZ, second, 0)

    def third(z, _):
        c = cour[z]
        hit = jnp.where(source_depth == z, jnp.float32(1.0), jnp.float32(0.0))
        two = lap(pad2, z)
        lap2[z] = two
        p3 = 2.0 * pad2[z + 4, 8:40, :] - pad1[z + 4, 8:40, :] + c * two + hit * plane_two
        pad3[z + 4, 8:40, :] = p3
        wave_out[z] = p3
        a2 = 2.0 * q3[z] - q4[z] + lap(padc3, z)
        q2[z] = a2
        padc2[z + 4, 8:40, :] = c * a2
        return 0

    lax.fori_loop(0, AZ, third, 0)

    def fourth(z, _):
        q1 = 2.0 * q2[z] - q3[z] + lap(padc2, z)
        adj_out[z] = q1
        g = q1 * lap0[z] + q2[z] * lap1[z] + q3[z] * lap2[z] + q4[z] * lap(pad3, z)
        g = pltpu.roll(g, ahead, 1)
        doubled[z, 0:AX, :] = g
        doubled[z, AX : 2 * AX, :] = g
        return 0

    lax.fori_loop(0, AZ, fourth, 0)

    def rolled(d):
        index = jnp.clip(d + lag, 0, K - 1)
        return doubled[pl.ds(index * SLAB, SLAB), pl.ds(AX - my_cross, AX), :]

    for d in OFFSETS:
        gsend[d + REACH] = rolled(d)

        @pl.when(there(d))
        def _(d=d):
            g_copy(d).start()

    grecv[REACH] = rolled(0)
    total[...] = jnp.zeros_like(total)

    def add_piece(offset):
        sender = jnp.clip(me + offset, 0, n - 1)
        cross, along = anchor[sender, 0], anchor[sender, 1]
        gap = me - cover[sender]
        covered = jnp.where((gap >= 0) & (gap < K), 1, 0)
        for i in range(2):
            for j in range(2):
                row_ok = rows >= cross if i == 0 else rows < cross
                lane_ok = lanes >= along if j == 0 else lanes < along
                ok = row_ok & lane_ok & (covered + jnp.zeros_like(rows) > 0)
                view = total.at[:, AX * i : AX * (i + 1), AY * j : AY * (j + 1)]
                view[...] = view[...] + jnp.where(ok, grecv[offset + REACH], 0.0)

    add_piece(0)
    for d in (1, -1, 2, -2, 3, -3):

        @pl.when(there(d))
        def _(d=d):
            g_copy(-d).wait_recv()
            add_piece(d)

    largest = jnp.zeros((8, AY), jnp.float32)
    for z in range(SLAB):
        sg = jnp.float32(2.0 * STEP_RATIO * STEP_RATIO) * vel[z] * total[z]
        total[z] = sg
        mag = jnp.abs(sg)
        mag = jnp.maximum(mag[:, 0:AY], mag[:, AY : 2 * AY])
        mag = mag.reshape(8, 8, AY).max(0)
        largest = jnp.maximum(largest, mag)

    base = 0
    waits = []
    for index, (stride, radix) in enumerate(stages):
        mxsend[index] = largest
        copies = []
        for j in range(1, radix):
            copies.append(
                pltpu.make_async_remote_copy(
                    src_ref=mxsend.at[index],
                    dst_ref=mxrecv.at[base + j - 1],
                    send_sem=ms_sem.at[base + j - 1],
                    recv_sem=mr_sem.at[base + j - 1],
                    device_id=(partner(stride, radix, j),),
                    device_id_type=MESH,
                )
            )
        for copy in copies:
            copy.start()
        for j, copy in enumerate(copies):
            copy.wait_recv()
            largest = jnp.maximum(largest, mxrecv[base + j])
        waits += copies
        base += radix - 1

    peak = jnp.max(largest) + jnp.float32(EPSILON)
    for z in range(SLAB):
        grad_out[z] = total[z] / peak

    for d in OFFSETS:

        @pl.when(there(d))
        def _(d=d):
            v_copy(d).wait_send()
            g_copy(d).wait_send()

    for copy in waits:
        copy.wait_send()


def shards(n, vel, prev, now, adj4, adj3, wavelet, spos, cover, anchor):
    stages = stages_of(n)
    partners = sum(radix - 1 for _, radix in stages)
    f32 = jnp.float32
    any_spec = pl.BlockSpec(memory_space=pl.ANY)
    vmem = pl.BlockSpec(memory_space=pltpu.VMEM)
    smem = pl.BlockSpec(memory_space=pltpu.SMEM)
    field = pltpu.VMEM((AZ, AX, AY), f32)
    padded = pltpu.VMEM((AZ + 8, AX + 16, AY), f32)
    pieces = pltpu.VMEM((SLOTS, SLAB, AX, AY), f32)
    dma = pltpu.SemaphoreType.DMA
    return pl.pallas_call(
        functools.partial(kernel, n, stages),
        out_shape=(
            jax.ShapeDtypeStruct((AZ, AX, AY), f32),
            jax.ShapeDtypeStruct((AZ, AX, AY), f32),
            jax.ShapeDtypeStruct(vel.shape, f32),
        ),
        in_specs=[vmem] + [any_spec] * 4 + [smem] * 4,
        out_specs=(vmem, vmem, vmem),
        scratch_shapes=[padded] * 6
        + [field] * 7
        + [pltpu.VMEM((AZ, 2 * AX, AY), f32)]
        + [pieces] * 4
        + [
            pltpu.VMEM(vel.shape, f32),
            pltpu.VMEM((len(stages), 8, AY), f32),
            pltpu.VMEM((partners, 8, AY), f32),
            dma((4,)),
            dma((SLOTS,)),
            dma((SLOTS,)),
            dma((SLOTS,)),
            dma((SLOTS,)),
            dma((partners,)),
            dma((partners,)),
        ],
        compiler_params=pltpu.CompilerParams(
            collective_id=0, has_side_effects=True, vmem_limit_bytes=48 * 1024 * 1024
        ),
    )(vel, prev, now, adj4, adj3, wavelet, spos, cover, anchor)


def solution(mesh):
    cube, pair = P("dev", None, None), P("dev", None)
    return jax.shard_map(
        functools.partial(shards, mesh.shape["dev"]),
        mesh=mesh,
        in_specs=(cube, cube, cube, cube, cube, pair, pair, P(), P()),
        out_specs=(cube, cube, cube),
        check_vma=False,
    )
```

```python
import functools

import jax
import jax.numpy as jnp
from jax import lax
from jax.experimental import pallas as pl
from jax.experimental.pallas import tpu as pltpu
from jax.sharding import PartitionSpec as P

SLAB = 8
K = 4
AX = 32
AY = 128
AZ = 32

WEIGHTS = (-205.0 / 72.0, 8.0 / 5.0, -1.0 / 5.0, 8.0 / 315.0, -1.0 / 560.0)
STEP_RATIO = 0.088
EPSILON = 1e-06
REACH = K - 1
HALF = SLAB // 2
SLOTS = 2 * REACH + 1
OFFSETS = (3, -3, 2, -2, 1, -1)
MESH = pl.DeviceIdType.MESH


def stages_of(count):
    stages, stride = [], 1
    while stride < count:
        left = count // stride
        radix = max(r for r in range(2, max(9, left + 1)) if left % r == 0 and (r <= 8 or r == left))
        if radix > 8:
            radix = next((r for r in range(8, 1, -1) if left % r == 0), left)
        stages.append((stride, radix))
        stride *= radix
    return stages


def kernel(
    n,
    stages,
    vel_in,
    prev_in,
    now_in,
    adj4_in,
    adj3_in,
    wavelet,
    spos,
    cover,
    anchor,
    wave_hbm,
    adj_hbm,
    grad_out,
    vel,
    wave_out,
    adj_out,
    pad0,
    pad1,
    pad2,
    pad3,
    padc3,
    padc2,
    q4,
    q3,
    q2,
    lap0,
    lap1,
    lap2,
    cour,
    doubled,
    vsend,
    vrecv,
    gsend,
    grecv,
    total,
    mxsend,
    mxrecv,
    in_sem,
    out_sem,
    vs_sem,
    vr_sem,
    gs_sem,
    gr_sem,
    ms_sem,
    mr_sem,
):
    me = lax.axis_index("dev")
    vel_load = pltpu.make_async_copy(vel_in, vel, in_sem.at[4])
    vel_load.start()
    barrier = pltpu.get_barrier_semaphore()
    group = stages[0][1]

    def there(d):
        return (me + d >= 0) & (me + d < n)

    def partner(stride, radix, j):
        digit = (me // stride) % radix
        return me + ((digit + j) % radix - digit) * stride

    expected = 0
    for stride, radix in stages:
        for j in range(1, radix):
            pl.semaphore_signal(
                barrier, inc=1, device_id=(partner(stride, radix, j),), device_id_type=MESH
            )
            expected += 1
    for d in OFFSETS:
        outside = there(d) & ((me + d + group) // group != (me + group) // group)

        @pl.when(outside)
        def _(d=d):
            pl.semaphore_signal(barrier, inc=1, device_id=(me + d,), device_id_type=MESH)

        expected = expected + jnp.where(outside, 1, 0)

    loads = [
        pltpu.make_async_copy(prev_in, pad0.at[4:36, 8:40], in_sem.at[0]),
        pltpu.make_async_copy(now_in, pad1.at[4:36, 8:40], in_sem.at[1]),
        pltpu.make_async_copy(adj4_in, q4, in_sem.at[2]),
        pltpu.make_async_copy(adj3_in, q3, in_sem.at[3]),
    ]
    for load in loads:
        load.start()

    rows = lax.broadcasted_iota(jnp.int32, (AX, AY), 0)
    lanes = lax.broadcasted_iota(jnp.int32, (AX, AY), 1)

    def fold(target):
        cross, along = anchor[target, 0], anchor[target, 1]
        low_lane = lanes >= along
        low_row = rows >= cross
        top = jnp.where(low_lane, vel[:, 0:AX, 0:AY], vel[:, 0:AX, AY : 2 * AY])
        bottom = jnp.where(low_lane, vel[:, AX : 2 * AX, 0:AY], vel[:, AX : 2 * AX, AY : 2 * AY])
        return jnp.where(low_row, top, bottom)

    vel_load.wait()
    for d in OFFSETS:
        vsend[d + REACH] = fold(jnp.clip(me + d, 0, n - 1))
    vrecv[REACH] = fold(me)

    pl.semaphore_wait(barrier, expected)

    def v_copy(d):
        return pltpu.make_async_remote_copy(
            src_ref=vsend.at[d + REACH],
            dst_ref=vrecv.at[REACH - d],
            send_sem=vs_sem.at[d + REACH],
            recv_sem=vr_sem.at[REACH - d],
            device_id=(me + d,),
            device_id_type=MESH,
        )

    def g_copy(d, half):
        planes = pl.ds(half * HALF, HALF)
        return pltpu.make_async_remote_copy(
            src_ref=gsend.at[d + REACH, planes],
            dst_ref=grecv.at[REACH - d, planes],
            send_sem=gs_sem.at[half, d + REACH],
            recv_sem=gr_sem.at[half, REACH - d],
            device_id=(me + d,),
            device_id_type=MESH,
        )

    for d in OFFSETS:

        @pl.when(there(d))
        def _(d=d):
            v_copy(d).start()

    for ref in (pad0, pad1, pad2, pad3, padc3, padc2):
        side = jnp.zeros((4, 48, AY), jnp.float32)
        ref[0:4] = side
        ref[36:40] = side

    def clear(z, _):
        edge = jnp.zeros((8, AY), jnp.float32)
        for ref in (pad0, pad1, pad2, pad3, padc3, padc2):
            ref[z + 4, 0:8, :] = edge
            ref[z + 4, 40:48, :] = edge
        return 0

    lax.fori_loop(0, AZ, clear, 0, unroll=2)

    lane_row = lax.broadcasted_iota(jnp.int32, (8, AY), 1)
    ups = [jnp.where(lane_row >= k, jnp.float32(WEIGHTS[k]), 0.0) for k in range(1, 5)]
    downs = [jnp.where(lane_row < AY - k, jnp.float32(WEIGHTS[k]), 0.0) for k in range(1, 5)]

    def lap(ref, z):
        parts = []
        for r in range(8, 40, 8):
            centre = ref[z + 4, r : r + 8, :]
            summed = jnp.float32(3.0 * WEIGHTS[0]) * centre
            for k in range(1, 5):
                summed = summed + jnp.float32(WEIGHTS[k]) * (
                    (ref[z + 4 + k, r : r + 8, :] + ref[z + 4 - k, r : r + 8, :])
                    + (ref[z + 4, r + k : r + k + 8, :] + ref[z + 4, r - k : r - k + 8, :])
                )
                summed = summed + (
                    pltpu.roll(centre, k, 1) * ups[k - 1]
                    + pltpu.roll(centre, AY - k, 1) * downs[k - 1]
                )
            parts.append(summed)
        return jnp.concatenate(parts, 0)

    for load in loads:
        load.wait()

    def first(z, _):
        lap0[z] = lap(pad0, z)
        lap1[z] = lap(pad1, z)
        return 0

    lax.fori_loop(0, AZ, first, 0, unroll=2)

    my_cross, my_along = anchor[me, 0], anchor[me, 1]
    lag = jnp.clip(me - cover[me], 0, K - 1)
    back = lax.rem(AY - my_along, AY)
    ahead = lax.rem(my_along, AY)

    for d in OFFSETS:

        @pl.when(there(d))
        def _(d=d):
            v_copy(-d).wait_recv()

    for k in range(K):
        piece = vrecv[REACH - lag + k]
        speed = pltpu.roll(piece.reshape(SLAB * AX, AY), back, 1) * jnp.float32(STEP_RATIO)
        speed = (speed * speed).reshape(SLAB, AX, AY)
        doubled[SLAB * k : SLAB * (k + 1), 0:AX, :] = speed
        doubled[SLAB * k : SLAB * (k + 1), AX : 2 * AX, :] = speed

    plane_hit = (rows == spos[0, 1]) & (lanes == spos[0, 2])
    plane_one = jnp.where(plane_hit, wavelet[0, 0], 0.0)
    plane_two = jnp.where(plane_hit, wavelet[0, 1], 0.0)
    source_depth = spos[0, 0]

    def second(z, _):
        c = doubled[z, pl.ds(my_cross, AX), :]
        cour[z] = c
        hit = jnp.where(source_depth == z, jnp.float32(1.0), jnp.float32(0.0))
        pad2[z + 4, 8:40, :] = (
            2.0 * pad1[z + 4, 8:40, :] - pad0[z + 4, 8:40, :] + c * lap1[z] + hit * plane_one
        )
        padc3[z + 4, 8:40, :] = c * q3[z]
        return 0

    lax.fori_loop(0, AZ, second, 0, unroll=4)

    def third(z, _):
        c = cour[z]
        hit = jnp.where(source_depth == z, jnp.float32(1.0), jnp.float32(0.0))
        two = lap(pad2, z)
        lap2[z] = two
        p3 = 2.0 * pad2[z + 4, 8:40, :] - pad1[z + 4, 8:40, :] + c * two + hit * plane_two
        pad3[z + 4, 8:40, :] = p3
        wave_out[z] = p3
        a2 = 2.0 * q3[z] - q4[z] + lap(padc3, z)
        q2[z] = a2
        padc2[z + 4, 8:40, :] = c * a2
        return 0

    lax.fori_loop(0, AZ, third, 0, unroll=2)
    wave_store = pltpu.make_async_copy(wave_out, wave_hbm, out_sem.at[0])
    adj_store = pltpu.make_async_copy(adj_out, adj_hbm, out_sem.at[1])
    wave_store.start()

    def fourth(step, half):
        z = (step // HALF) * SLAB + half * HALF + lax.rem(step, HALF)
        q1 = 2.0 * q2[z] - q3[z] + lap(padc2, z)
        adj_out[z] = q1
        g = q1 * lap0[z] + q2[z] * lap1[z] + q3[z] * lap2[z] + q4[z] * lap(pad3, z)
        g = pltpu.roll(g, ahead, 1)
        doubled[z, 0:AX, :] = g
        doubled[z, AX : 2 * AX, :] = g
        return half

    def rolled(d, half):
        index = jnp.clip(d + lag, 0, K - 1)
        return doubled[pl.ds(index * SLAB + half * HALF, HALF), pl.ds(AX - my_cross, AX), :]

    for half in range(2):
        planes = slice(half * HALF, (half + 1) * HALF)
        lax.fori_loop(0, AZ // 2, fourth, half, unroll=2)
        for d in OFFSETS:
            gsend[d + REACH, planes] = rolled(d, half)

            @pl.when(there(d))
            def _(d=d, half=half):
                g_copy(d, half).start()

        grecv[REACH, planes] = rolled(0, half)

    adj_store.start()
    total[...] = jnp.zeros_like(total)

    def add_piece(offset):
        sender = jnp.clip(me + offset, 0, n - 1)
        cross, along = anchor[sender, 0], anchor[sender, 1]
        gap = me - cover[sender]
        covered = jnp.where((gap >= 0) & (gap < K), 1, 0)
        for i in range(2):
            for j in range(2):
                row_ok = rows >= cross if i == 0 else rows < cross
                lane_ok = lanes >= along if j == 0 else lanes < along
                ok = row_ok & lane_ok & (covered + jnp.zeros_like(rows) > 0)
                view = total.at[:, AX * i : AX * (i + 1), AY * j : AY * (j + 1)]
                view[...] = view[...] + jnp.where(ok, grecv[offset + REACH], 0.0)

    add_piece(0)
    for d in (1, -1, 2, -2, 3, -3):

        @pl.when(there(d))
        def _(d=d):
            g_copy(-d, 0).wait_recv()
            g_copy(-d, 1).wait_recv()
            add_piece(d)

    largest = jnp.zeros((8, AY), jnp.float32)
    for z in range(SLAB):
        sg = jnp.float32(2.0 * STEP_RATIO * STEP_RATIO) * vel[z] * total[z]
        total[z] = sg
        mag = jnp.abs(sg)
        mag = jnp.maximum(mag[:, 0:AY], mag[:, AY : 2 * AY])
        mag = mag.reshape(8, 8, AY).max(0)
        largest = jnp.maximum(largest, mag)

    base = 0
    waits = []
    for index, (stride, radix) in enumerate(stages):
        mxsend[index] = largest
        copies = []
        for j in range(1, radix):
            copies.append(
                pltpu.make_async_remote_copy(
                    src_ref=mxsend.at[index],
                    dst_ref=mxrecv.at[base + j - 1],
                    send_sem=ms_sem.at[base + j - 1],
                    recv_sem=mr_sem.at[base + j - 1],
                    device_id=(partner(stride, radix, j),),
                    device_id_type=MESH,
                )
            )
        for copy in copies:
            copy.start()
        for j, copy in enumerate(copies):
            copy.wait_recv()
            largest = jnp.maximum(largest, mxrecv[base + j])
        waits += copies
        base += radix - 1

    peak = jnp.max(largest) + jnp.float32(EPSILON)
    for z in range(SLAB):
        grad_out[z] = total[z] / peak

    for d in OFFSETS:

        @pl.when(there(d))
        def _(d=d):
            v_copy(d).wait_send()
            g_copy(d, 0).wait_send()
            g_copy(d, 1).wait_send()

    wave_store.wait()
    adj_store.wait()
    for copy in waits:
        copy.wait_send()


def shards(n, vel, prev, now, adj4, adj3, wavelet, spos, cover, anchor):
    stages = stages_of(n)
    partners = sum(radix - 1 for _, radix in stages)
    f32 = jnp.float32
    hbm = pl.BlockSpec(memory_space=pltpu.HBM)
    vmem = pl.BlockSpec(memory_space=pltpu.VMEM)
    smem = pl.BlockSpec(memory_space=pltpu.SMEM)
    field = pltpu.VMEM((AZ, AX, AY), f32)
    padded = pltpu.VMEM((AZ + 8, AX + 16, AY), f32)
    pieces = pltpu.VMEM((SLOTS, SLAB, AX, AY), f32)
    dma = pltpu.SemaphoreType.DMA
    return pl.pallas_call(
        functools.partial(kernel, n, stages),
        out_shape=(
            jax.ShapeDtypeStruct((AZ, AX, AY), f32),
            jax.ShapeDtypeStruct((AZ, AX, AY), f32),
            jax.ShapeDtypeStruct(vel.shape, f32),
        ),
        in_specs=[hbm] * 5 + [smem] * 4,
        out_specs=(hbm, hbm, vmem),
        scratch_shapes=[pltpu.VMEM(vel.shape, f32), field, field]
        + [padded] * 6
        + [field] * 7
        + [pltpu.VMEM((AZ, 2 * AX, AY), f32)]
        + [pieces] * 4
        + [
            pltpu.VMEM(vel.shape, f32),
            pltpu.VMEM((len(stages), 8, AY), f32),
            pltpu.VMEM((partners, 8, AY), f32),
            dma((5,)),
            dma((2,)),
            dma((SLOTS,)),
            dma((SLOTS,)),
            dma((2, SLOTS)),
            dma((2, SLOTS)),
            dma((partners,)),
            dma((partners,)),
        ],
        compiler_params=pltpu.CompilerParams(
            collective_id=0, has_side_effects=True, vmem_limit_bytes=60 * 1024 * 1024
        ),
    )(vel, prev, now, adj4, adj3, wavelet, spos, cover, anchor)


def solution(mesh):
    cube, pair = P("dev", None, None), P("dev", None)
    return jax.shard_map(
        functools.partial(shards, mesh.shape["dev"]),
        mesh=mesh,
        in_specs=(cube, cube, cube, cube, cube, pair, pair, P(), P()),
        out_specs=(cube, cube, cube),
        check_vma=False,
    )
```

```python
import functools

import jax
import jax.numpy as jnp
from jax import lax
from jax.experimental import pallas as pl
from jax.experimental.pallas import tpu as pltpu
from jax.sharding import PartitionSpec as P

SLAB = 8
K = 4
AX = 32
AY = 128
AZ = 32

WEIGHTS = (-205.0 / 72.0, 8.0 / 5.0, -1.0 / 5.0, 8.0 / 315.0, -1.0 / 560.0)
STEP_RATIO = 0.088
EPSILON = 1e-06
REACH = K - 1
HALF = SLAB // 2
SLOTS = 2 * REACH + 1
OFFSETS = (3, -3, 2, -2, 1, -1)
MESH = pl.DeviceIdType.MESH


def stages_of(count):
    stages, stride = [], 1
    while stride < count:
        left = count // stride
        radix = max(r for r in range(2, max(9, left + 1)) if left % r == 0 and (r <= 8 or r == left))
        if radix > 8:
            radix = next((r for r in range(8, 1, -1) if left % r == 0), left)
        stages.append((stride, radix))
        stride *= radix
    return stages


def kernel(
    n,
    stages,
    vel_in,
    prev_in,
    now_in,
    adj4_in,
    adj3_in,
    wavelet,
    spos,
    cover,
    anchor,
    wave_hbm,
    adj_hbm,
    grad_out,
    vel,
    wave_out,
    adj_out,
    pad0,
    pad1,
    pad2,
    pad3,
    padc3,
    padc2,
    q4,
    q3,
    q2,
    lap0,
    lap1,
    lap2,
    cour,
    doubled,
    vsend,
    vrecv,
    gsend,
    grecv,
    total,
    mxsend,
    mxrecv,
    in_sem,
    out_sem,
    vs_sem,
    vr_sem,
    gs_sem,
    gr_sem,
    ms_sem,
    mr_sem,
):
    me = lax.axis_index("dev")
    vel_load = pltpu.make_async_copy(vel_in, vel, in_sem.at[4])
    vel_load.start()
    barrier = pltpu.get_barrier_semaphore()
    group = stages[0][1]

    def there(d):
        return (me + d >= 0) & (me + d < n)

    def partner(stride, radix, j):
        digit = (me // stride) % radix
        return me + ((digit + j) % radix - digit) * stride

    expected = 0
    for stride, radix in stages:
        for j in range(1, radix):
            pl.semaphore_signal(
                barrier, inc=1, device_id=(partner(stride, radix, j),), device_id_type=MESH
            )
            expected += 1
    for d in OFFSETS:
        outside = there(d) & ((me + d + group) // group != (me + group) // group)

        @pl.when(outside)
        def _(d=d):
            pl.semaphore_signal(barrier, inc=1, device_id=(me + d,), device_id_type=MESH)

        expected = expected + jnp.where(outside, 1, 0)

    loads = [
        pltpu.make_async_copy(prev_in, pad0.at[4:36, 8:40], in_sem.at[0]),
        pltpu.make_async_copy(now_in, pad1.at[4:36, 8:40], in_sem.at[1]),
        pltpu.make_async_copy(adj4_in, q4, in_sem.at[2]),
        pltpu.make_async_copy(adj3_in, q3, in_sem.at[3]),
    ]
    for load in loads:
        load.start()

    rows = lax.broadcasted_iota(jnp.int32, (AX, AY), 0)
    lanes = lax.broadcasted_iota(jnp.int32, (AX, AY), 1)

    def fold(target):
        cross, along = anchor[0, target], anchor[1, target]
        low_lane = lanes >= along
        low_row = rows >= cross
        top = jnp.where(low_lane, vel[:, 0:AX, 0:AY], vel[:, 0:AX, AY : 2 * AY])
        bottom = jnp.where(low_lane, vel[:, AX : 2 * AX, 0:AY], vel[:, AX : 2 * AX, AY : 2 * AY])
        return jnp.where(low_row, top, bottom)

    vel_load.wait()
    for d in OFFSETS:
        vsend[d + REACH] = fold(jnp.clip(me + d, 0, n - 1))
    vrecv[REACH] = fold(me)

    pl.semaphore_wait(barrier, expected)

    def v_copy(d):
        return pltpu.make_async_remote_copy(
            src_ref=vsend.at[d + REACH],
            dst_ref=vrecv.at[REACH - d],
            send_sem=vs_sem.at[d + REACH],
            recv_sem=vr_sem.at[REACH - d],
            device_id=(me + d,),
            device_id_type=MESH,
        )

    def g_copy(d, half):
        planes = pl.ds(half * HALF, HALF)
        return pltpu.make_async_remote_copy(
            src_ref=gsend.at[d + REACH, planes],
            dst_ref=grecv.at[REACH - d, planes],
            send_sem=gs_sem.at[half, d + REACH],
            recv_sem=gr_sem.at[half, REACH - d],
            device_id=(me + d,),
            device_id_type=MESH,
        )

    for d in OFFSETS:

        @pl.when(there(d))
        def _(d=d):
            v_copy(d).start()

    for ref in (pad0, pad1, pad2, pad3, padc3, padc2):
        side = jnp.zeros((4, 48, AY), jnp.float32)
        ref[0:4] = side
        ref[36:40] = side

    def clear(z, _):
        edge = jnp.zeros((8, AY), jnp.float32)
        for ref in (pad0, pad1, pad2, pad3, padc3, padc2):
            ref[z + 4, 0:8, :] = edge
            ref[z + 4, 40:48, :] = edge
        return 0

    lax.fori_loop(0, AZ, clear, 0, unroll=2)

    lane_row = lax.broadcasted_iota(jnp.int32, (8, AY), 1)
    ups = [jnp.where(lane_row >= k, jnp.float32(WEIGHTS[k]), 0.0) for k in range(1, 5)]
    downs = [jnp.where(lane_row < AY - k, jnp.float32(WEIGHTS[k]), 0.0) for k in range(1, 5)]

    def lap(ref, z):
        parts = []
        for r in range(8, 40, 8):
            centre = ref[z + 4, r : r + 8, :]
            summed = jnp.float32(3.0 * WEIGHTS[0]) * centre
            for k in range(1, 5):
                summed = summed + jnp.float32(WEIGHTS[k]) * (
                    (ref[z + 4 + k, r : r + 8, :] + ref[z + 4 - k, r : r + 8, :])
                    + (ref[z + 4, r + k : r + k + 8, :] + ref[z + 4, r - k : r - k + 8, :])
                )
                summed = summed + (
                    pltpu.roll(centre, k, 1) * ups[k - 1]
                    + pltpu.roll(centre, AY - k, 1) * downs[k - 1]
                )
            parts.append(summed)
        return jnp.concatenate(parts, 0)

    for load in loads:
        load.wait()

    def first(z, _):
        lap0[z] = lap(pad0, z)
        lap1[z] = lap(pad1, z)
        return 0

    lax.fori_loop(0, AZ, first, 0, unroll=4)

    my_cross, my_along = anchor[0, me], anchor[1, me]
    lag = jnp.clip(me - cover[me], 0, K - 1)
    back = lax.rem(AY - my_along, AY)
    ahead = lax.rem(my_along, AY)

    for d in OFFSETS:

        @pl.when(there(d))
        def _(d=d):
            v_copy(-d).wait_recv()

    for k in range(K):
        piece = vrecv[REACH - lag + k]
        speed = pltpu.roll(piece.reshape(SLAB * AX, AY), back, 1) * jnp.float32(STEP_RATIO)
        speed = (speed * speed).reshape(SLAB, AX, AY)
        doubled[SLAB * k : SLAB * (k + 1), 0:AX, :] = speed
        doubled[SLAB * k : SLAB * (k + 1), AX : 2 * AX, :] = speed

    plane_hit = (rows == spos[0, 1]) & (lanes == spos[0, 2])
    plane_one = jnp.where(plane_hit, wavelet[0, 0], 0.0)
    plane_two = jnp.where(plane_hit, wavelet[0, 1], 0.0)
    source_depth = spos[0, 0]

    def second(z, _):
        c = doubled[z, pl.ds(my_cross, AX), :]
        cour[z] = c
        hit = jnp.where(source_depth == z, jnp.float32(1.0), jnp.float32(0.0))
        pad2[z + 4, 8:40, :] = (
            2.0 * pad1[z + 4, 8:40, :] - pad0[z + 4, 8:40, :] + c * lap1[z] + hit * plane_one
        )
        padc3[z + 4, 8:40, :] = c * q3[z]
        return 0

    lax.fori_loop(0, AZ, second, 0, unroll=4)

    def third(z, _):
        c = cour[z]
        hit = jnp.where(source_depth == z, jnp.float32(1.0), jnp.float32(0.0))
        two = lap(pad2, z)
        lap2[z] = two
        p3 = 2.0 * pad2[z + 4, 8:40, :] - pad1[z + 4, 8:40, :] + c * two + hit * plane_two
        pad3[z + 4, 8:40, :] = p3
        wave_out[z] = p3
        a2 = 2.0 * q3[z] - q4[z] + lap(padc3, z)
        q2[z] = a2
        padc2[z + 4, 8:40, :] = c * a2
        return 0

    lax.fori_loop(0, AZ, third, 0, unroll=4)
    wave_store = pltpu.make_async_copy(wave_out, wave_hbm, out_sem.at[0])
    adj_store = pltpu.make_async_copy(adj_out, adj_hbm, out_sem.at[1])
    wave_store.start()

    def fourth(step, half):
        z = (step // HALF) * SLAB + half * HALF + lax.rem(step, HALF)
        q1 = 2.0 * q2[z] - q3[z] + lap(padc2, z)
        adj_out[z] = q1
        g = q1 * lap0[z] + q2[z] * lap1[z] + q3[z] * lap2[z] + q4[z] * lap(pad3, z)
        g = pltpu.roll(g, ahead, 1)
        doubled[z, 0:AX, :] = g
        doubled[z, AX : 2 * AX, :] = g
        return half

    def rolled(d, half):
        index = jnp.clip(d + lag, 0, K - 1)
        return doubled[pl.ds(index * SLAB + half * HALF, HALF), pl.ds(AX - my_cross, AX), :]

    for half in range(2):
        planes = slice(half * HALF, (half + 1) * HALF)
        lax.fori_loop(0, AZ // 2, fourth, half, unroll=4)
        for d in OFFSETS:
            gsend[d + REACH, planes] = rolled(d, half)

            @pl.when(there(d))
            def _(d=d, half=half):
                g_copy(d, half).start()

        grecv[REACH, planes] = rolled(0, half)

    adj_store.start()
    total[...] = jnp.zeros_like(total)

    def add_piece(offset):
        sender = jnp.clip(me + offset, 0, n - 1)
        cross, along = anchor[0, sender], anchor[1, sender]
        gap = me - cover[sender]
        covered = jnp.where((gap >= 0) & (gap < K), 1, 0)
        for i in range(2):
            for j in range(2):
                row_ok = rows >= cross if i == 0 else rows < cross
                lane_ok = lanes >= along if j == 0 else lanes < along
                ok = row_ok & lane_ok & (covered + jnp.zeros_like(rows) > 0)
                view = total.at[:, AX * i : AX * (i + 1), AY * j : AY * (j + 1)]
                view[...] = view[...] + jnp.where(ok, grecv[offset + REACH], 0.0)

    add_piece(0)
    for d in (1, -1, 2, -2, 3, -3):

        @pl.when(there(d))
        def _(d=d):
            g_copy(-d, 0).wait_recv()
            g_copy(-d, 1).wait_recv()
            add_piece(d)

    largest = jnp.zeros((8, AY), jnp.float32)
    for z in range(SLAB):
        sg = jnp.float32(2.0 * STEP_RATIO * STEP_RATIO) * vel[z] * total[z]
        total[z] = sg
        mag = jnp.abs(sg)
        mag = jnp.maximum(mag[:, 0:AY], mag[:, AY : 2 * AY])
        mag = mag.reshape(8, 8, AY).max(0)
        largest = jnp.maximum(largest, mag)

    base = 0
    waits = []
    for index, (stride, radix) in enumerate(stages):
        mxsend[index] = largest
        copies = []
        for j in range(1, radix):
            copies.append(
                pltpu.make_async_remote_copy(
                    src_ref=mxsend.at[index],
                    dst_ref=mxrecv.at[base + j - 1],
                    send_sem=ms_sem.at[base + j - 1],
                    recv_sem=mr_sem.at[base + j - 1],
                    device_id=(partner(stride, radix, j),),
                    device_id_type=MESH,
                )
            )
        for copy in copies:
            copy.start()
        for j, copy in enumerate(copies):
            copy.wait_recv()
            largest = jnp.maximum(largest, mxrecv[base + j])
        waits += copies
        base += radix - 1

    peak = jnp.max(largest) + jnp.float32(EPSILON)
    for z in range(SLAB):
        grad_out[z] = total[z] / peak

    for d in OFFSETS:

        @pl.when(there(d))
        def _(d=d):
            v_copy(d).wait_send()
            g_copy(d, 0).wait_send()
            g_copy(d, 1).wait_send()

    wave_store.wait()
    adj_store.wait()
    for copy in waits:
        copy.wait_send()


def shards(n, vel, prev, now, adj4, adj3, wavelet, spos, cover, anchor):
    stages = stages_of(n)
    partners = sum(radix - 1 for _, radix in stages)
    f32 = jnp.float32
    hbm = pl.BlockSpec(memory_space=pltpu.HBM)
    vmem = pl.BlockSpec(memory_space=pltpu.VMEM)
    smem = pl.BlockSpec(memory_space=pltpu.SMEM)
    field = pltpu.VMEM((AZ, AX, AY), f32)
    padded = pltpu.VMEM((AZ + 8, AX + 16, AY), f32)
    pieces = pltpu.VMEM((SLOTS, SLAB, AX, AY), f32)
    dma = pltpu.SemaphoreType.DMA
    return pl.pallas_call(
        functools.partial(kernel, n, stages),
        out_shape=(
            jax.ShapeDtypeStruct((AZ, AX, AY), f32),
            jax.ShapeDtypeStruct((AZ, AX, AY), f32),
            jax.ShapeDtypeStruct(vel.shape, f32),
        ),
        in_specs=[hbm] * 5 + [smem] * 4,
        out_specs=(hbm, hbm, vmem),
        scratch_shapes=[pltpu.VMEM(vel.shape, f32), field, field]
        + [padded] * 6
        + [field] * 7
        + [pltpu.VMEM((AZ, 2 * AX, AY), f32)]
        + [pieces] * 4
        + [
            pltpu.VMEM(vel.shape, f32),
            pltpu.VMEM((len(stages), 8, AY), f32),
            pltpu.VMEM((partners, 8, AY), f32),
            dma((5,)),
            dma((2,)),
            dma((SLOTS,)),
            dma((SLOTS,)),
            dma((2, SLOTS)),
            dma((2, SLOTS)),
            dma((partners,)),
            dma((partners,)),
        ],
        compiler_params=pltpu.CompilerParams(
            collective_id=0, has_side_effects=True, vmem_limit_bytes=60 * 1024 * 1024
        ),
    )(vel, prev, now, adj4, adj3, wavelet, spos, cover, anchor.T)


def solution(mesh):
    cube, pair = P("dev", None, None), P("dev", None)
    return jax.shard_map(
        functools.partial(shards, mesh.shape["dev"]),
        mesh=mesh,
        in_specs=(cube, cube, cube, cube, cube, pair, pair, P(), P()),
        out_specs=(cube, cube, cube),
        check_vma=False,
    )
```

```python
import functools

import jax
import jax.numpy as jnp
from jax import lax
from jax.experimental import pallas as pl
from jax.experimental.pallas import tpu as pltpu
from jax.sharding import PartitionSpec as P

SLAB = 8
K = 4
AX = 32
AY = 128
AZ = 32

WEIGHTS = (-205.0 / 72.0, 8.0 / 5.0, -1.0 / 5.0, 8.0 / 315.0, -1.0 / 560.0)
STEP_RATIO = 0.088
EPSILON = 1e-06
REACH = K - 1
PARTS = 4
HALF = SLAB // PARTS
SLOTS = 2 * REACH + 1
OFFSETS = (3, -3, 2, -2, 1, -1)
MESH = pl.DeviceIdType.MESH


def stages_of(count):
    stages, stride = [], 1
    while stride < count:
        left = count // stride
        radix = max(r for r in range(2, max(9, left + 1)) if left % r == 0 and (r <= 8 or r == left))
        if radix > 8:
            radix = next((r for r in range(8, 1, -1) if left % r == 0), left)
        stages.append((stride, radix))
        stride *= radix
    return stages


def kernel(
    n,
    stages,
    vel_in,
    prev_in,
    now_in,
    adj4_in,
    adj3_in,
    wavelet,
    spos,
    cover,
    anchor,
    wave_hbm,
    adj_hbm,
    grad_out,
    vel,
    wave_out,
    adj_out,
    pad0,
    pad1,
    pad2,
    pad3,
    padc3,
    padc2,
    q4,
    q3,
    q2,
    lap0,
    lap1,
    lap2,
    cour,
    doubled,
    vsend,
    vrecv,
    gsend,
    grecv,
    total,
    mxsend,
    mxrecv,
    in_sem,
    out_sem,
    vs_sem,
    vr_sem,
    gs_sem,
    gr_sem,
    ms_sem,
    mr_sem,
):
    me = lax.axis_index("dev")
    vel_load = pltpu.make_async_copy(vel_in, vel, in_sem.at[4])
    vel_load.start()
    barrier = pltpu.get_barrier_semaphore()
    group = stages[0][1]

    def there(d):
        return (me + d >= 0) & (me + d < n)

    def partner(stride, radix, j):
        digit = (me // stride) % radix
        return me + ((digit + j) % radix - digit) * stride

    expected = 0
    for stride, radix in stages:
        for j in range(1, radix):
            pl.semaphore_signal(
                barrier, inc=1, device_id=(partner(stride, radix, j),), device_id_type=MESH
            )
            expected += 1
    for d in OFFSETS:
        outside = there(d) & ((me + d + group) // group != (me + group) // group)

        @pl.when(outside)
        def _(d=d):
            pl.semaphore_signal(barrier, inc=1, device_id=(me + d,), device_id_type=MESH)

        expected = expected + jnp.where(outside, 1, 0)

    loads = [
        pltpu.make_async_copy(prev_in, pad0.at[4:36, 8:40], in_sem.at[0]),
        pltpu.make_async_copy(now_in, pad1.at[4:36, 8:40], in_sem.at[1]),
        pltpu.make_async_copy(adj4_in, q4, in_sem.at[2]),
        pltpu.make_async_copy(adj3_in, q3, in_sem.at[3]),
    ]
    for load in loads:
        load.start()

    rows = lax.broadcasted_iota(jnp.int32, (AX, AY), 0)
    lanes = lax.broadcasted_iota(jnp.int32, (AX, AY), 1)

    def fold(target):
        cross, along = anchor[0, target], anchor[1, target]
        low_lane = lanes >= along
        low_row = rows >= cross
        top = jnp.where(low_lane, vel[:, 0:AX, 0:AY], vel[:, 0:AX, AY : 2 * AY])
        bottom = jnp.where(low_lane, vel[:, AX : 2 * AX, 0:AY], vel[:, AX : 2 * AX, AY : 2 * AY])
        return jnp.where(low_row, top, bottom)

    vel_load.wait()
    for d in OFFSETS:
        vsend[d + REACH] = fold(jnp.clip(me + d, 0, n - 1))
    vrecv[REACH] = fold(me)

    pl.semaphore_wait(barrier, expected)

    def v_copy(d):
        return pltpu.make_async_remote_copy(
            src_ref=vsend.at[d + REACH],
            dst_ref=vrecv.at[REACH - d],
            send_sem=vs_sem.at[d + REACH],
            recv_sem=vr_sem.at[REACH - d],
            device_id=(me + d,),
            device_id_type=MESH,
        )

    def g_copy(d, half):
        planes = pl.ds(half * HALF, HALF)
        return pltpu.make_async_remote_copy(
            src_ref=gsend.at[d + REACH, planes],
            dst_ref=grecv.at[REACH - d, planes],
            send_sem=gs_sem.at[half, d + REACH],
            recv_sem=gr_sem.at[half, REACH - d],
            device_id=(me + d,),
            device_id_type=MESH,
        )

    for d in OFFSETS:

        @pl.when(there(d))
        def _(d=d):
            v_copy(d).start()

    for ref in (pad0, pad1, pad2, pad3, padc3, padc2):
        side = jnp.zeros((4, 48, AY), jnp.float32)
        ref[0:4] = side
        ref[36:40] = side

    def clear(z, _):
        edge = jnp.zeros((8, AY), jnp.float32)
        for ref in (pad0, pad1, pad2, pad3, padc3, padc2):
            ref[z + 4, 0:8, :] = edge
            ref[z + 4, 40:48, :] = edge
        return 0

    lax.fori_loop(0, AZ, clear, 0, unroll=2)

    lane_row = lax.broadcasted_iota(jnp.int32, (8, AY), 1)
    ups = [jnp.where(lane_row >= k, jnp.float32(WEIGHTS[k]), 0.0) for k in range(1, 5)]
    downs = [jnp.where(lane_row < AY - k, jnp.float32(WEIGHTS[k]), 0.0) for k in range(1, 5)]

    def lap(ref, z):
        parts = []
        for r in range(8, 40, 8):
            centre = ref[z + 4, r : r + 8, :]
            summed = jnp.float32(3.0 * WEIGHTS[0]) * centre
            for k in range(1, 5):
                summed = summed + jnp.float32(WEIGHTS[k]) * (
                    (ref[z + 4 + k, r : r + 8, :] + ref[z + 4 - k, r : r + 8, :])
                    + (ref[z + 4, r + k : r + k + 8, :] + ref[z + 4, r - k : r - k + 8, :])
                )
                summed = summed + (
                    pltpu.roll(centre, k, 1) * ups[k - 1]
                    + pltpu.roll(centre, AY - k, 1) * downs[k - 1]
                )
            parts.append(summed)
        return jnp.concatenate(parts, 0)

    for load in loads:
        load.wait()

    def first(z, _):
        lap0[z] = lap(pad0, z)
        lap1[z] = lap(pad1, z)
        return 0

    lax.fori_loop(0, AZ, first, 0, unroll=4)

    my_cross, my_along = anchor[0, me], anchor[1, me]
    lag = jnp.clip(me - cover[me], 0, K - 1)
    back = lax.rem(AY - my_along, AY)
    ahead = lax.rem(my_along, AY)

    for d in OFFSETS:

        @pl.when(there(d))
        def _(d=d):
            v_copy(-d).wait_recv()

    for k in range(K):
        piece = vrecv[REACH - lag + k]
        speed = pltpu.roll(piece.reshape(SLAB * AX, AY), back, 1) * jnp.float32(STEP_RATIO)
        speed = (speed * speed).reshape(SLAB, AX, AY)
        doubled[SLAB * k : SLAB * (k + 1), 0:AX, :] = speed
        doubled[SLAB * k : SLAB * (k + 1), AX : 2 * AX, :] = speed

    plane_hit = (rows == spos[0, 1]) & (lanes == spos[0, 2])
    plane_one = jnp.where(plane_hit, wavelet[0, 0], 0.0)
    plane_two = jnp.where(plane_hit, wavelet[0, 1], 0.0)
    source_depth = spos[0, 0]

    def second(z, _):
        c = doubled[z, pl.ds(my_cross, AX), :]
        cour[z] = c
        hit = jnp.where(source_depth == z, jnp.float32(1.0), jnp.float32(0.0))
        pad2[z + 4, 8:40, :] = (
            2.0 * pad1[z + 4, 8:40, :] - pad0[z + 4, 8:40, :] + c * lap1[z] + hit * plane_one
        )
        padc3[z + 4, 8:40, :] = c * q3[z]
        return 0

    lax.fori_loop(0, AZ, second, 0, unroll=4)

    def third(z, _):
        c = cour[z]
        hit = jnp.where(source_depth == z, jnp.float32(1.0), jnp.float32(0.0))
        two = lap(pad2, z)
        lap2[z] = two
        p3 = 2.0 * pad2[z + 4, 8:40, :] - pad1[z + 4, 8:40, :] + c * two + hit * plane_two
        pad3[z + 4, 8:40, :] = p3
        wave_out[z] = p3
        a2 = 2.0 * q3[z] - q4[z] + lap(padc3, z)
        q2[z] = a2
        padc2[z + 4, 8:40, :] = c * a2
        return 0

    lax.fori_loop(0, AZ, third, 0, unroll=4)
    wave_store = pltpu.make_async_copy(wave_out, wave_hbm, out_sem.at[0])
    adj_store = pltpu.make_async_copy(adj_out, adj_hbm, out_sem.at[1])
    wave_store.start()

    def fourth(step, half):
        z = (step // HALF) * SLAB + half * HALF + lax.rem(step, HALF)
        q1 = 2.0 * q2[z] - q3[z] + lap(padc2, z)
        adj_out[z] = q1
        g = q1 * lap0[z] + q2[z] * lap1[z] + q3[z] * lap2[z] + q4[z] * lap(pad3, z)
        g = pltpu.roll(g, ahead, 1)
        doubled[z, 0:AX, :] = g
        doubled[z, AX : 2 * AX, :] = g
        return half

    def rolled(d, half):
        index = jnp.clip(d + lag, 0, K - 1)
        return doubled[pl.ds(index * SLAB + half * HALF, HALF), pl.ds(AX - my_cross, AX), :]

    for half in range(PARTS):
        planes = slice(half * HALF, (half + 1) * HALF)
        lax.fori_loop(0, AZ // PARTS, fourth, half, unroll=4)
        for d in OFFSETS:
            gsend[d + REACH, planes] = rolled(d, half)

            @pl.when(there(d))
            def _(d=d, half=half):
                g_copy(d, half).start()

        grecv[REACH, planes] = rolled(0, half)

    adj_store.start()
    total[...] = jnp.zeros_like(total)

    def add_piece(offset):
        sender = jnp.clip(me + offset, 0, n - 1)
        cross, along = anchor[0, sender], anchor[1, sender]
        gap = me - cover[sender]
        covered = jnp.where((gap >= 0) & (gap < K), 1, 0)
        for i in range(2):
            for j in range(2):
                row_ok = rows >= cross if i == 0 else rows < cross
                lane_ok = lanes >= along if j == 0 else lanes < along
                ok = row_ok & lane_ok & (covered + jnp.zeros_like(rows) > 0)
                view = total.at[:, AX * i : AX * (i + 1), AY * j : AY * (j + 1)]
                view[...] = view[...] + jnp.where(ok, grecv[offset + REACH], 0.0)

    add_piece(0)
    for d in (1, -1, 2, -2, 3, -3):

        @pl.when(there(d))
        def _(d=d):
            for half in range(PARTS):
                g_copy(-d, half).wait_recv()
            add_piece(d)

    largest = jnp.zeros((8, AY), jnp.float32)
    for z in range(SLAB):
        sg = jnp.float32(2.0 * STEP_RATIO * STEP_RATIO) * vel[z] * total[z]
        total[z] = sg
        mag = jnp.abs(sg)
        mag = jnp.maximum(mag[:, 0:AY], mag[:, AY : 2 * AY])
        mag = mag.reshape(8, 8, AY).max(0)
        largest = jnp.maximum(largest, mag)

    base = 0
    waits = []
    for index, (stride, radix) in enumerate(stages):
        mxsend[index] = largest
        copies = []
        for j in range(1, radix):
            copies.append(
                pltpu.make_async_remote_copy(
                    src_ref=mxsend.at[index],
                    dst_ref=mxrecv.at[base + j - 1],
                    send_sem=ms_sem.at[base + j - 1],
                    recv_sem=mr_sem.at[base + j - 1],
                    device_id=(partner(stride, radix, j),),
                    device_id_type=MESH,
                )
            )
        for copy in copies:
            copy.start()
        for j, copy in enumerate(copies):
            copy.wait_recv()
            largest = jnp.maximum(largest, mxrecv[base + j])
        waits += copies
        base += radix - 1

    peak = jnp.max(largest) + jnp.float32(EPSILON)
    for z in range(SLAB):
        grad_out[z] = total[z] / peak

    for d in OFFSETS:

        @pl.when(there(d))
        def _(d=d):
            v_copy(d).wait_send()
            for half in range(PARTS):
                g_copy(d, half).wait_send()

    wave_store.wait()
    adj_store.wait()
    for copy in waits:
        copy.wait_send()


def shards(n, vel, prev, now, adj4, adj3, wavelet, spos, cover, anchor):
    stages = stages_of(n)
    partners = sum(radix - 1 for _, radix in stages)
    f32 = jnp.float32
    hbm = pl.BlockSpec(memory_space=pltpu.HBM)
    vmem = pl.BlockSpec(memory_space=pltpu.VMEM)
    smem = pl.BlockSpec(memory_space=pltpu.SMEM)
    field = pltpu.VMEM((AZ, AX, AY), f32)
    padded = pltpu.VMEM((AZ + 8, AX + 16, AY), f32)
    pieces = pltpu.VMEM((SLOTS, SLAB, AX, AY), f32)
    dma = pltpu.SemaphoreType.DMA
    return pl.pallas_call(
        functools.partial(kernel, n, stages),
        out_shape=(
            jax.ShapeDtypeStruct((AZ, AX, AY), f32),
            jax.ShapeDtypeStruct((AZ, AX, AY), f32),
            jax.ShapeDtypeStruct(vel.shape, f32),
        ),
        in_specs=[hbm] * 5 + [smem] * 4,
        out_specs=(hbm, hbm, vmem),
        scratch_shapes=[pltpu.VMEM(vel.shape, f32), field, field]
        + [padded] * 6
        + [field] * 7
        + [pltpu.VMEM((AZ, 2 * AX, AY), f32)]
        + [pieces] * 4
        + [
            pltpu.VMEM(vel.shape, f32),
            pltpu.VMEM((len(stages), 8, AY), f32),
            pltpu.VMEM((partners, 8, AY), f32),
            dma((5,)),
            dma((2,)),
            dma((SLOTS,)),
            dma((SLOTS,)),
            dma((PARTS, SLOTS)),
            dma((PARTS, SLOTS)),
            dma((partners,)),
            dma((partners,)),
        ],
        compiler_params=pltpu.CompilerParams(
            collective_id=0, has_side_effects=True, vmem_limit_bytes=60 * 1024 * 1024
        ),
    )(vel, prev, now, adj4, adj3, wavelet, spos, cover, anchor.T)


def solution(mesh):
    cube, pair = P("dev", None, None), P("dev", None)
    return jax.shard_map(
        functools.partial(shards, mesh.shape["dev"]),
        mesh=mesh,
        in_specs=(cube, cube, cube, cube, cube, pair, pair, P(), P()),
        out_specs=(cube, cube, cube),
        check_vma=False,
    )
```
